512 devices in a mesh: row: 4 (over z_hi), col: 64 (over z_lo, x, y), section: 2 (over core).
Axes of the slice: x: 4, y: 8, z: 8 (z_hi: 4, z_lo: 2; z = z_hi * 2 + z_lo), core: 2. Of those that a mesh axis runs over, the one named last changes fastest.
Arguments:
- block_vals: bfloat16 [512, 4, 512, 512], P(('row', 'col', 'section')), may hold values from 0.0099487305 to 1
- present: int32 [512, 4], P(('row', 'col', 'section')), may hold values 0 or 1
- kept_rows: int32 [512, 2], replicated, may hold values from 0 to 3, as said below
- column_owner: int32 [262144, 1], P(('row', 'col', 'section')), may hold values from 0 to 127; in each aligned block of 512 rows (0 to 511, 512 to 1023, ...) at most 8 rows name the same one
Outputs:
- pruned: bfloat16 [4, 128, 128, 8, 1024], P('row', ('col', 'section'))
- arrived: int32 [4, 128, 128, 8], P('row', ('col', 'section'))
The draws below stay inside these ranges and needn't reach their ends.
Inputs may be any that keep to these rules, and one draw needn't show every extreme that they name: kept_rows[J, 0] is the block column's own position J // 128; kept_rows[J, 1] is another position of its cluster. `column_owner`: among the 512 matrix columns of one block column at most 8 have the same owner, and in every draw some owner receives exactly 8 from some block column.
All inputs are finite; a program needn't handle non-finite values. No bound on the sum of `present` on one device may be relied on, other than what follows from the above.
Results may differ from the reference program's by a relative error of at most 0.02.
Values may be sent and summed in bfloat16 or wider, within the bound.
No kernel may reach another device: no remote copies, remote signals or barrier semaphores. Data moves between devices by JAX's collectives and lax.ppermute only.
A program may use at most 64 MiB of HBM per device.

```python
import math
import jax
import jax.numpy as jnp
import numpy as np
from jax import lax

B = 512
K = 4
KEEP = 2
CLUSTERS = 128
NB = 512
CAP = 8


def draw_kept_rows(key, part):
    key = jax.random.fold_in(key, 7)
    index = jnp.arange(NB, dtype=jnp.int32)
    own_place = index // CLUSTERS
    offset = jax.random.randint(key, (NB,), 1, K, dtype=jnp.int32)
    other_place = (own_place + offset) % K
    return jnp.stack([own_place, other_place], axis=1).astype(jnp.int32)


def place_ends(values, key, least, high):
    spot = [jax.random.randint(jax.random.fold_in(key, axis), (), 0, length) for axis, length in enumerate(values.shape)]
    widest = values.shape.index(max(values.shape))
    next_to = spot[:widest] + [(spot[widest] + 1) % values.shape[widest]] + spot[widest + 1:]
    return values.at[tuple(spot)].set(least).at[tuple(next_to)].set(high)


def shard_levels(rng, dims, shards, smallest, top_value):
    def one(axis_at, parts):
        steps = jax.random.uniform(jax.random.fold_in(jax.random.fold_in(rng, 6), axis_at), (parts,), jnp.float32, smallest / len(shards), top_value / len(shards))
        return jnp.repeat(jnp.exp(steps), dims[axis_at] // parts).reshape((-1,) + (1,) * (len(dims) - axis_at - 1))

    loudness = one(*shards[0])
    for cut in shards[1:]:
        loudness = loudness * one(*cut)
    return loudness


def shared_out(rng, own, number, rows, count, top, reach, slope):
    order = jax.random.permutation(rng, count)
    crowded, ordinary = portions_of(count, rows * top, reach, slope, True), portions_of(count, rows * top, reach, slope, False)
    places = jnp.arange(count)

    def named(lengths, rotation):
        used = int((lengths > 0).sum())
        fixed = max(1, used // 4)
        moved = fixed + (places - fixed + rotation * (used - fixed)) % max(1, count - fixed)
        return jnp.zeros((count,), jnp.int32).at[order[jnp.where(places < fixed, places, moved)]].set(jnp.asarray(lengths, jnp.int32))

    lengths = jnp.where(number % 4 == 0, named(crowded, number // 4), named(ordinary, number - number // 4 - 1))
    mixed = jax.random.permutation(jax.random.fold_in(own, 3), count)
    giver, taker = mixed[0:count // 2 * 2:2], mixed[1:count // 2 * 2:2]
    room = jnp.minimum(lengths[giver] - 1, reach - lengths[taker]) // 2
    room = jnp.where((giver == order[0]) | (taker == order[0]) | (lengths[taker] == 0), 0, jnp.maximum(room, 0))
    moved = jax.random.randint(jax.random.fold_in(own, 4), (count // 2,), 0, 1 << 20) % (room + 1)
    lengths = lengths.at[giver].add(-moved).at[taker].add(moved)
    items = jnp.searchsorted(jnp.cumsum(lengths), jnp.arange(rows * top), side="right").astype(jnp.int32)
    grid = items.reshape(top, rows).T
    grid = grid[jax.random.permutation(jax.random.fold_in(own, 1), rows)]
    rotation = jax.random.randint(jax.random.fold_in(own, 2), (rows, 1), 0, top)
    return jnp.take_along_axis(grid, (jnp.arange(top)[None, :] + rotation) % top, axis=1)


def portions_of(number_of, total, bound, lean, full):
    loads = [(1 << 20) // math.isqrt(grade ** lean) + 1 for grade in range(1, number_of + 1)]
    largest = bound if full else min(bound, max(-(-total // number_of), total * loads[0] // sum(loads)))
    least = 1 if total - largest >= number_of - 1 else 0
    holding, rest = [largest] + [least] * (number_of - 1), total - largest - least * (number_of - 1)
    while rest > 0:
        free = [i for i in range(1, number_of) if holding[i] < largest] or [i for i in range(1, number_of) if holding[i] < bound]
        pool, remaining = sum([loads[i] for i in free]), rest
        for i in free:
            more = min(bound - holding[i], max(1, remaining * loads[i] // pool), rest)
            holding[i] = holding[i] + more
            rest = rest - more
    return np.array(holding)


def setup_inputs(seed: int = 0) -> dict:
    arg_keys = jax.random.split(jax.random.key(seed), 5)
    block_vals = jnp.clip(jnp.exp(math.log(1.0) - 4.61031033 * jax.random.uniform(arg_keys[0], (NB, K, B, B), jnp.float32) ** shard_levels(arg_keys[0], (NB, K, B, B), ((0, 512),), -0.2, 0.2)), 0.0099487305, 1.0).astype(jnp.bfloat16)
    present = place_ends((jax.random.randint(arg_keys[1], (NB, K), 0, 4) < 3).astype(jnp.int32), jax.random.fold_in(arg_keys[1], 1), 0, 1)
    kept_rows = draw_kept_rows(jax.random.fold_in(arg_keys[4], 71), 0)
    column_owner_keys = jax.random.split(jax.random.fold_in(arg_keys[3], 1), (NB * B) // B)
    column_owner_turns = jax.random.permutation(jax.random.fold_in(arg_keys[3], 3), (NB * B) // B)
    column_owner = jax.vmap(lambda own, number: shared_out(jax.random.fold_in(arg_keys[3], 2), own, number, B, CLUSTERS, 1, CAP, 2))(column_owner_keys, column_owner_turns).reshape((NB * B, 1))
    return dict(block_vals=block_vals, present=present, kept_rows=kept_rows, column_owner=column_owner)


def cluster_columns(block_vals, present, kept_rows, cluster):
    positions = jnp.arange(K, dtype=jnp.int32)
    members = positions * CLUSTERS + cluster
    column_set = jnp.take(block_vals, members, axis=0)
    live_mask = jnp.logical_or(jnp.take(present, members, axis=0) > 0, positions[:, None] == positions[None, :])
    effective = jnp.where(live_mask[:, :, None, None], column_set, jnp.zeros_like(column_set))
    kept_local = jnp.take(kept_rows, members, axis=0)
    left_blocks = effective[:, kept_local]
    products = jnp.einsum("tjmik,jtke->jtemi", left_blocks.astype(jnp.float32), effective.astype(jnp.float32))
    rounded = lax.optimization_barrier(products.astype(jnp.bfloat16))
    expanded = jnp.sum(rounded.astype(jnp.float32), axis=1)
    inflated = expanded * expanded
    column_mean = jnp.mean(inflated, axis=(2, 3)) + 1e-6
    normalized = inflated / column_mean[:, :, None, None]
    return normalized.astype(jnp.bfloat16).reshape(K, B, KEEP * B)


def reference(block_vals, present, kept_rows, column_owner):
    def one_cluster(cluster):
        return cluster_columns(block_vals, present, kept_rows, cluster)

    per_cluster = lax.map(one_cluster, jnp.arange(CLUSTERS, dtype=jnp.int32))
    columns = jnp.transpose(per_cluster, (1, 0, 2, 3)).reshape(NB * B, KEEP * B)
    owners = column_owner[:, 0].astype(jnp.int32)
    owner_hits = (owners.reshape(NB, B)[:, :, None] == jnp.arange(CLUSTERS, dtype=jnp.int32)[None, None, :]).astype(jnp.int32)
    earlier = jnp.cumsum(owner_hits, axis=1) - owner_hits
    order_in = jnp.sum(earlier * owner_hits, axis=2).reshape(-1).astype(jnp.int32)
    index = jnp.arange(NB * B, dtype=jnp.int32)
    block_index = index // B
    row_place = block_index // CLUSTERS
    source = block_index % CLUSTERS
    pruned = jnp.zeros((K, CLUSTERS, CLUSTERS, CAP, KEEP * B), jnp.bfloat16)
    pruned = pruned.at[row_place, owners, source, order_in].set(columns)
    arrived = jnp.full((K, CLUSTERS, CLUSTERS, CAP), -1, jnp.int32)
    arrived = arrived.at[row_place, owners, source, order_in].set(index)
    return pruned, arrived
```

```python
import jax
import jax.numpy as jnp
from jax import lax
from jax.experimental import pallas as pl
from jax.experimental.pallas import tpu as pltpu
from jax.sharding import PartitionSpec as P

EPS = 1e-6
OWNERS = ("col", "section")


def finish_kernel(first_ref, second_ref, out_ref):
    half = first_ref.shape[-1]
    first = first_ref[...].astype(jnp.float32)
    second = second_ref[...].astype(jnp.float32)
    first = first * first
    second = second * second
    total = jnp.sum(first, axis=-1, keepdims=True) + jnp.sum(second, axis=-1, keepdims=True)
    mean = total * (1.0 / (2 * half)) + EPS
    out_ref[:, :half] = (first / mean).astype(out_ref.dtype)
    out_ref[:, half:] = (second / mean).astype(out_ref.dtype)


def finish(first, second):
    rows, half = first.shape
    step = min(rows, 128)
    spec = pl.BlockSpec((step, half), lambda i: (i, 0))
    return pl.pallas_call(
        finish_kernel,
        grid=(rows // step,),
        in_specs=[spec, spec],
        out_specs=pl.BlockSpec((step, 2 * half), lambda i: (i, 0)),
        out_shape=jax.ShapeDtypeStruct((rows, 2 * half), jnp.bfloat16),
        cost_estimate=pl.CostEstimate(
            flops=6 * rows * half, bytes_accessed=8 * rows * half, transcendentals=0
        ),
        name="finish",
    )(first, second)


def shards(block_vals, present, kept_rows, column_owner):
    size = block_vals.shape[-1]
    places = block_vals.shape[1]
    kept_count = kept_rows.shape[1]
    place = lax.axis_index("row")
    cluster = lax.axis_index("col") * lax.axis_size("section") + lax.axis_index("section")
    clusters = lax.axis_size("col") * lax.axis_size("section")
    capacity = size // lax.axis_size("col")
    slots = clusters * capacity

    def effective(at):
        block = lax.dynamic_index_in_dim(block_vals[0], at, 0, keepdims=False)
        live = jnp.logical_or(
            lax.dynamic_index_in_dim(present[0], at, 0, keepdims=False) > 0, at == place
        )
        return jnp.where(live, block, jnp.zeros_like(block))

    def kept(at, m):
        return kept_rows[at * clusters + cluster, m]

    def outgoing(m):
        return [effective(kept((place + d) % places, m)) for d in range(places)]

    def exchange(blocks):
        return [
            blocks[d]
            if d == 0
            else lax.ppermute(blocks[d], "row", [(i, (i + d) % places) for i in range(places)])
            for d in range(places)
        ]

    left_first = exchange(outgoing(0))

    owners = column_owner[:, 0]
    hits = owners[:, None] == jnp.arange(clusters, dtype=jnp.int32)[None, :]
    index = jnp.arange(size, dtype=jnp.int32)
    before = (index[:, None] > index[None, :]).astype(jnp.bfloat16)
    earlier = jnp.dot(before, hits.astype(jnp.bfloat16), preferred_element_type=jnp.float32)
    order = jnp.sum(jnp.where(hits, earlier, 0.0), axis=1).astype(jnp.int32)
    slot_of = owners * capacity + order
    chosen = jnp.arange(slots, dtype=jnp.int32)[:, None] == slot_of[None, :]
    source = jnp.max(jnp.where(chosen, index[None, :], -1), axis=1)
    ids = jnp.where(source >= 0, (place * clusters + cluster) * size + source, -1)
    arrived_ids = lax.all_to_all(
        ids.reshape(clusters, capacity), OWNERS, split_axis=0, concat_axis=0, tiled=True
    )

    pick = chosen.astype(jnp.bfloat16)
    right = [
        lax.dot_general(
            pick,
            effective((place - d) % places),
            (((1,), (1,)), ((), ())),
            preferred_element_type=jnp.float32,
        ).astype(jnp.bfloat16)
        for d in range(places)
    ]

    def products(left):
        total = None
        for a, b in zip(right, left):
            term = lax.dot_general(
                a, b, (((1,), (1,)), ((), ())), preferred_element_type=jnp.float32
            )
            total = term if total is None else total + term
        return total.astype(jnp.bfloat16)

    def to_owners(values):
        return lax.all_to_all(
            values.reshape(clusters, capacity, size), OWNERS, split_axis=0, concat_axis=0, tiled=True
        ).reshape(slots, size)

    second_out, left_first = lax.optimization_barrier((outgoing(1), left_first))
    left_second = exchange(second_out)
    first_sent = products(left_first)
    first = to_owners(first_sent)
    left_second, first = lax.optimization_barrier((left_second, first))
    second = to_owners(products(left_second))
    pruned = finish(first, second)
    return (
        pruned.reshape(1, 1, clusters, capacity, kept_count * size),
        arrived_ids.reshape(1, 1, clusters, capacity),
    )


def solution(mesh):
    placed = (
        P(("row", "col", "section"), None, None, None),
        P(("row", "col", "section"), None),
        P(),
        P(("row", "col", "section"), None),
    )
    return jax.shard_map(
        shards,
        mesh=mesh,
        in_specs=placed,
        out_specs=(
            P("row", ("col", "section"), None, None, None),
            P("row", ("col", "section"), None, None),
        ),
        check_vma=False,
    )
```

```python
import jax
import jax.numpy as jnp
from jax import lax
from jax.experimental import pallas as pl
from jax.experimental.pallas import tpu as pltpu
from jax.sharding import PartitionSpec as P

EPS = 1e-6
OWNERS = ("col", "section")
TILES = 4
CHUNKS = (((0, 0, 8),), ((1, 0, 8),))


def segments(chunk, size):
    out, at = [], 0
    for m, first, last in chunk:
        rows = (last - first) * size // 8
        out.append((m, first * size // 8, at, rows))
        at += rows
    return out, at


def own_cluster():
    return lax.axis_index("col") * lax.axis_size("section") + lax.axis_index("section")


def needed(m, target, present_ref, kept_ref):
    clusters = lax.axis_size("col") * lax.axis_size("section")
    block = target if m == 0 else kept_ref[m, target * clusters + own_cluster()]
    live = jnp.logical_or(present_ref[0, block] > 0, block == lax.axis_index("row"))
    return block, live


def stage_kernel(chunk, present_ref, kept_ref, blocks_ref, *refs):
    places, size = present_ref.shape[1], blocks_ref.shape[-1]
    outs, (held, in_sems, out_sems) = refs[:-3], refs[-3:]
    place = lax.axis_index("row")
    parts = segments(chunk, size)[0]
    loads = []
    for k in range(places - 1):
        target = lax.rem(place + k + 1, places)
        for i, (m, first, at, rows) in enumerate(parts):
            block, live = needed(m, target, present_ref, kept_ref)
            load = pltpu.make_async_copy(
                blocks_ref.at[0, block, pl.ds(first, rows)],
                held.at[k, pl.ds(at, rows)],
                in_sems.at[k, i],
            )
            loads.append((k, live, load))

            @pl.when(live)
            def _():
                load.start()

            @pl.when(jnp.logical_not(live))
            def _():
                held[k, at : at + rows, :] = jnp.zeros((rows, size), held.dtype)

    stores = [
        pltpu.make_async_copy(held.at[k], outs[k], out_sems.at[k]) for k in range(places - 1)
    ]
    for i, (k, live, load) in enumerate(loads):

        @pl.when(live)
        def _():
            load.wait()

        if i % len(parts) == len(parts) - 1:
            stores[k].start()
    for store in stores:
        store.wait()


def stage(chunk, block_vals, present, kept_rows):
    others, size = block_vals.shape[1] - 1, block_vals.shape[-1]
    rows = segments(chunk, size)[1]
    return pl.pallas_call(
        lambda *refs: stage_kernel(chunk, *refs),
        in_specs=[
            pl.BlockSpec(memory_space=pltpu.SMEM),
            pl.BlockSpec(memory_space=pltpu.SMEM),
            pl.BlockSpec(memory_space=pl.ANY),
        ],
        out_specs=[pl.BlockSpec(memory_space=pl.ANY)] * others,
        out_shape=[jax.ShapeDtypeStruct((rows, size), block_vals.dtype)] * others,
        scratch_shapes=[
            pltpu.VMEM((others, rows, size), block_vals.dtype),
            pltpu.SemaphoreType.DMA((others, len(chunk))),
            pltpu.SemaphoreType.DMA((others,)),
        ],
        cost_estimate=pl.CostEstimate(
            flops=0, bytes_accessed=4 * others * rows * size, transcendentals=0
        ),
        name="stage",
    )(present, kept_rows.T, block_vals)


def products_kernel(chunk, present_ref, kept_ref, slot_ref, blocks_ref, *refs):
    places, size = present_ref.shape[1], slot_ref.shape[1]
    lefts, out_ref = refs[:-1], refs[-1]
    place = lax.axis_index("row")
    own = []
    for m, first, _, rows in segments(chunk, size)[0]:
        block, live = needed(m, place, present_ref, kept_ref)
        part = blocks_ref[0, block, first : first + rows, :]
        own.append(jnp.where(live, part, jnp.zeros_like(part)))
    own = own[0] if len(own) == 1 else jnp.concatenate(own, axis=0)
    total = jnp.dot(own, blocks_ref[0, place], preferred_element_type=jnp.float32)
    for k in range(places - 1):
        at = lax.rem(place + places - 1 - k, places)
        live = present_ref[0, at] > 0
        term = jnp.dot(lefts[k][...], blocks_ref[0, at], preferred_element_type=jnp.float32)
        total = total + jnp.where(live, term, jnp.zeros_like(term))
    expanded = total.astype(jnp.bfloat16)
    slots = out_ref.shape[0]
    step = slots // TILES
    for i in range(TILES):
        here = i * step + lax.broadcasted_iota(jnp.int32, (step, size), 0)
        pick = jnp.where(here == slot_ref[...], 1.0, 0.0).astype(jnp.bfloat16)
        out_ref[i * step : (i + 1) * step, :] = lax.dot_general(
            pick, expanded, (((1,), (1,)), ((), ())), preferred_element_type=jnp.float32
        ).astype(out_ref.dtype)


def products(chunk, present, kept_rows, slot_of, block_vals, left, slots):
    size = block_vals.shape[-1]
    rows = left[0].shape[0]
    smem = pl.BlockSpec(memory_space=pltpu.SMEM)
    vmem = pl.BlockSpec(memory_space=pltpu.VMEM)
    return pl.pallas_call(
        lambda *refs: products_kernel(chunk, *refs),
        in_specs=[smem, smem, vmem, vmem] + [vmem] * len(left),
        out_specs=vmem,
        out_shape=jax.ShapeDtypeStruct((slots, rows), jnp.bfloat16),
        compiler_params=pltpu.CompilerParams(vmem_limit_bytes=32 * 2**20),
        cost_estimate=pl.CostEstimate(
            flops=50_000_000_000, bytes_accessed=8 * size * size, transcendentals=0
        ),
        name="products",
    )(present, kept_rows.T, slot_of.reshape(1, size), block_vals, *left)


def finish_kernel(*refs):
    count = len(CHUNKS)
    arrived, out_ref = refs[:count], refs[count]
    held, result, in_sems, out_sems = refs[count + 1 : 2 * count + 1], *refs[2 * count + 1 :]
    rows, wide = result.shape
    size = wide // 2
    step = rows // TILES
    loads = [
        [
            pltpu.make_async_copy(
                arrived[c].at[pl.ds(i * step, step)],
                held[c].at[pl.ds(i * step, step)],
                in_sems.at[c, i],
            )
            for c in range(count)
        ]
        for i in range(TILES)
    ]
    for tile in loads:
        for load in tile:
            load.start()
    stores = []
    for i in range(TILES):
        part = slice(i * step, (i + 1) * step)
        squares, total = [], 0.0
        for c in range(count):
            loads[i][c].wait()
            value = held[c][part, :].astype(jnp.float32)
            squares.append(value * value)
            total = total + jnp.sum(squares[c], axis=-1, keepdims=True)
        scale = 1.0 / (total * (1.0 / wide) + EPS)
        for c in range(count):
            for m, first, at, length in segments(CHUNKS[c], size)[0]:
                result[part, m * size + first : m * size + first + length] = (
                    squares[c][:, at : at + length] * scale
                ).astype(result.dtype)
        stores.append(
            pltpu.make_async_copy(
                result.at[pl.ds(i * step, step)], out_ref.at[pl.ds(i * step, step)], out_sems.at[i]
            )
        )
        stores[i].start()
    for store in stores:
        store.wait()


def finish(arrived, wide):
    rows = arrived[0].shape[0]
    return pl.pallas_call(
        finish_kernel,
        in_specs=[pl.BlockSpec(memory_space=pl.ANY)] * len(arrived),
        out_specs=pl.BlockSpec(memory_space=pltpu.HBM),
        out_shape=jax.ShapeDtypeStruct((rows, wide), jnp.bfloat16),
        scratch_shapes=[pltpu.VMEM(a.shape, a.dtype) for a in arrived]
        + [
            pltpu.VMEM((rows, wide), jnp.bfloat16),
            pltpu.SemaphoreType.DMA((len(arrived), TILES)),
            pltpu.SemaphoreType.DMA((TILES,)),
        ],
        compiler_params=pltpu.CompilerParams(vmem_limit_bytes=32 * 2**20),
        cost_estimate=pl.CostEstimate(
            flops=3 * rows * wide, bytes_accessed=4 * rows * wide, transcendentals=0
        ),
        name="finish",
    )(*arrived)


def shards(block_vals, present, kept_rows, column_owner):
    size = block_vals.shape[-1]
    places = block_vals.shape[1]
    kept_count = kept_rows.shape[1]
    place = lax.axis_index("row")
    cluster = lax.axis_index("col") * lax.axis_size("section") + lax.axis_index("section")
    clusters = lax.axis_size("col") * lax.axis_size("section")
    capacity = size // lax.axis_size("col")
    slots = clusters * capacity

    def exchange(blocks):
        return [
            lax.ppermute(block, "row", [(i, (i + k + 1) % places) for i in range(places)])
            for k, block in enumerate(blocks)
        ]

    def to_owners(values):
        values = values.reshape(clusters, capacity, -1)
        return lax.all_to_all(values, OWNERS, split_axis=0, concat_axis=0, tiled=True)

    staged = stage(CHUNKS[0], block_vals, present, kept_rows)
    owners, here, staged = lax.optimization_barrier((column_owner[:, 0], present, staged))
    left_first = exchange(staged)

    hits = owners[:, None] == jnp.arange(clusters, dtype=jnp.int32)[None, :]
    index = jnp.arange(size, dtype=jnp.int32)
    before = (index[:, None] > index[None, :]).astype(jnp.bfloat16)
    earlier = jnp.dot(before, hits.astype(jnp.bfloat16), preferred_element_type=jnp.float32)
    order = jnp.sum(jnp.where(hits, earlier, 0.0), axis=1).astype(jnp.int32)
    slot_of = owners * capacity + order
    chosen = jnp.arange(slots, dtype=jnp.int32)[:, None] == slot_of[None, :]
    source = jnp.max(jnp.where(chosen, index[None, :], -1), axis=1)
    ids = jnp.where(source >= 0, (place * clusters + cluster) * size + source, -1)
    ids, here = lax.optimization_barrier((ids, here))
    arrived_ids = lax.all_to_all(
        ids.reshape(clusters, capacity), OWNERS, split_axis=0, concat_axis=0, tiled=True
    )

    left_second = exchange(stage(CHUNKS[1], block_vals, here, kept_rows))
    first = products(CHUNKS[0], present, kept_rows, slot_of, block_vals, left_first, slots)
    slot_later = lax.optimization_barrier((first, slot_of))[1]
    first = to_owners(first)
    second = to_owners(
        products(CHUNKS[1], present, kept_rows, slot_later, block_vals, left_second, slots)
    )
    arrived = [first.reshape(slots, -1), second.reshape(slots, -1)]
    pruned = finish(arrived, kept_count * size)
    return (
        pruned.reshape(1, 1, clusters, capacity, kept_count * size),
        arrived_ids.reshape(1, 1, clusters, capacity),
    )


def solution(mesh):
    placed = (
        P(("row", "col", "section"), None, None, None),
        P(("row", "col", "section"), None),
        P(),
        P(("row", "col", "section"), None),
    )
    return jax.shard_map(
        shards,
        mesh=mesh,
        in_specs=placed,
        out_specs=(
            P("row", ("col", "section"), None, None, None),
            P("row", ("col", "section"), None, None),
        ),
        check_vma=False,
    )
```

```python
import jax
import jax.numpy as jnp
from jax import lax
from jax.experimental import pallas as pl
from jax.experimental.pallas import tpu as pltpu
from jax.sharding import PartitionSpec as P

EPS = 1e-6
OWNERS = ("col", "section")
TILES = 4
CHUNKS = (((0, 0, 8),), ((1, 0, 8),))


def segments(chunk, size):
    out, at = [], 0
    for m, first, last in chunk:
        rows = (last - first) * size // 8
        out.append((m, first * size // 8, at, rows))
        at += rows
    return out, at


def own_cluster():
    return lax.axis_index("col") * lax.axis_size("section") + lax.axis_index("section")


def needed(m, target, present_ref, kept_ref):
    clusters = lax.axis_size("col") * lax.axis_size("section")
    block = target if m == 0 else kept_ref[m, target * clusters + own_cluster()]
    live = jnp.logical_or(present_ref[0, block] > 0, block == lax.axis_index("row"))
    return block, live


def stage_kernel(chunk, present_ref, kept_ref, blocks_ref, *refs):
    places, size = present_ref.shape[1], blocks_ref.shape[-1]
    outs, (held, in_sems, out_sems) = refs[:-3], refs[-3:]
    place = lax.axis_index("row")
    parts = segments(chunk, size)[0]
    loads = []
    for k in range(places - 1):
        target = lax.rem(place + k + 1, places)
        for i, (m, first, at, rows) in enumerate(parts):
            block, live = needed(m, target, present_ref, kept_ref)
            load = pltpu.make_async_copy(
                blocks_ref.at[0, block, pl.ds(first, rows)],
                held.at[k, pl.ds(at, rows)],
                in_sems.at[k, i],
            )
            loads.append((k, live, load))

            @pl.when(live)
            def _():
                load.start()

            @pl.when(jnp.logical_not(live))
            def _():
                held[k, at : at + rows, :] = jnp.zeros((rows, size), held.dtype)

    stores = [
        pltpu.make_async_copy(held.at[k], outs[k], out_sems.at[k]) for k in range(places - 1)
    ]
    for i, (k, live, load) in enumerate(loads):

        @pl.when(live)
        def _():
            load.wait()

        if i % len(parts) == len(parts) - 1:
            stores[k].start()
    for store in stores:
        store.wait()


def stage(chunk, block_vals, present, kept_rows):
    others, size = block_vals.shape[1] - 1, block_vals.shape[-1]
    rows = segments(chunk, size)[1]
    return pl.pallas_call(
        lambda *refs: stage_kernel(chunk, *refs),
        in_specs=[
            pl.BlockSpec(memory_space=pltpu.SMEM),
            pl.BlockSpec(memory_space=pltpu.SMEM),
            pl.BlockSpec(memory_space=pl.ANY),
        ],
        out_specs=[pl.BlockSpec(memory_space=pl.ANY)] * others,
        out_shape=[jax.ShapeDtypeStruct((rows, size), block_vals.dtype)] * others,
        scratch_shapes=[
            pltpu.VMEM((others, rows, size), block_vals.dtype),
            pltpu.SemaphoreType.DMA((others, len(chunk))),
            pltpu.SemaphoreType.DMA((others,)),
        ],
        cost_estimate=pl.CostEstimate(
            flops=0, bytes_accessed=4 * others * rows * size, transcendentals=0
        ),
        name="stage",
    )(present, kept_rows.T, block_vals)


def products_kernel(chunk, present_ref, kept_ref, slot_ref, blocks_ref, *refs):
    places, size = present_ref.shape[1], slot_ref.shape[1]
    lefts, out_ref = refs[:-1], refs[-1]
    place = lax.axis_index("row")
    own = []
    for m, first, _, rows in segments(chunk, size)[0]:
        block, live = needed(m, place, present_ref, kept_ref)
        part = blocks_ref[0, block, first : first + rows, :]
        own.append(jnp.where(live, part, jnp.zeros_like(part)))
    own = own[0] if len(own) == 1 else jnp.concatenate(own, axis=0)
    total = jnp.dot(own, blocks_ref[0, place], preferred_element_type=jnp.float32)
    for k in range(places - 1):
        at = lax.rem(place + places - 1 - k, places)
        live = present_ref[0, at] > 0
        term = jnp.dot(lefts[k][...], blocks_ref[0, at], preferred_element_type=jnp.float32)
        total = total + jnp.where(live, term, jnp.zeros_like(term))
    expanded = total.astype(jnp.bfloat16)
    slots = out_ref.shape[0]
    step = slots // TILES
    for i in range(TILES):
        here = i * step + lax.broadcasted_iota(jnp.int32, (step, size), 0)
        pick = jnp.where(here == slot_ref[...], 1.0, 0.0).astype(jnp.bfloat16)
        out_ref[i * step : (i + 1) * step, :] = lax.dot_general(
            pick, expanded, (((1,), (1,)), ((), ())), preferred_element_type=jnp.float32
        ).astype(out_ref.dtype)


def products(chunk, present, kept_rows, slot_of, block_vals, left, slots):
    size = block_vals.shape[-1]
    rows = left[0].shape[0]
    smem = pl.BlockSpec(memory_space=pltpu.SMEM)
    vmem = pl.BlockSpec(memory_space=pltpu.VMEM)
    return pl.pallas_call(
        lambda *refs: products_kernel(chunk, *refs),
        in_specs=[smem, smem, vmem, vmem] + [vmem] * len(left),
        out_specs=vmem,
        out_shape=jax.ShapeDtypeStruct((slots, rows), jnp.bfloat16),
        compiler_params=pltpu.CompilerParams(vmem_limit_bytes=62 * 2**20),
        cost_estimate=pl.CostEstimate(
            flops=50_000_000_000, bytes_accessed=8 * size * size, transcendentals=0
        ),
        name="products",
    )(present, kept_rows.T, slot_of.reshape(1, size), block_vals, *left)


def finish_kernel(*refs):
    count = len(CHUNKS)
    arrived, out_ref = refs[:count], refs[count]
    held, result, in_sems, out_sems = refs[count + 1 : 2 * count + 1], *refs[2 * count + 1 :]
    rows, wide = result.shape
    size = wide // 2
    step = rows // TILES
    loads = [
        [
            pltpu.make_async_copy(
                arrived[c].at[pl.ds(i * step, step)],
                held[c].at[pl.ds(i * step, step)],
                in_sems.at[c, i],
            )
            for c in range(count)
        ]
        for i in range(TILES)
    ]
    for tile in loads:
        for load in tile:
            load.start()
    stores = []
    for i in range(TILES):
        part = slice(i * step, (i + 1) * step)
        squares, total = [], 0.0
        for c in range(count):
            loads[i][c].wait()
            value = held[c][part, :].astype(jnp.float32)
            squares.append(value * value)
            total = total + jnp.sum(squares[c], axis=-1, keepdims=True)
        scale = 1.0 / (total * (1.0 / wide) + EPS)
        for c in range(count):
            for m, first, at, length in segments(CHUNKS[c], size)[0]:
                result[part, m * size + first : m * size + first + length] = (
                    squares[c][:, at : at + length] * scale
                ).astype(result.dtype)
        stores.append(
            pltpu.make_async_copy(
                result.at[pl.ds(i * step, step)], out_ref.at[pl.ds(i * step, step)], out_sems.at[i]
            )
        )
        stores[i].start()
    for store in stores:
        store.wait()


def finish(arrived, wide):
    rows = arrived[0].shape[0]
    return pl.pallas_call(
        finish_kernel,
        in_specs=[pl.BlockSpec(memory_space=pl.ANY)] * len(arrived),
        out_specs=pl.BlockSpec(memory_space=pltpu.HBM),
        out_shape=jax.ShapeDtypeStruct((rows, wide), jnp.bfloat16),
        scratch_shapes=[pltpu.VMEM(a.shape, a.dtype) for a in arrived]
        + [
            pltpu.VMEM((rows, wide), jnp.bfloat16),
            pltpu.SemaphoreType.DMA((len(arrived), TILES)),
            pltpu.SemaphoreType.DMA((TILES,)),
        ],
        compiler_params=pltpu.CompilerParams(vmem_limit_bytes=62 * 2**20),
        cost_estimate=pl.CostEstimate(
            flops=3 * rows * wide, bytes_accessed=4 * rows * wide, transcendentals=0
        ),
        name="finish",
    )(*arrived)


def shards(block_vals, present, kept_rows, column_owner):
    size = block_vals.shape[-1]
    places = block_vals.shape[1]
    kept_count = kept_rows.shape[1]
    place = lax.axis_index("row")
    cluster = lax.axis_index("col") * lax.axis_size("section") + lax.axis_index("section")
    clusters = lax.axis_size("col") * lax.axis_size("section")
    capacity = size // lax.axis_size("col")
    slots = clusters * capacity

    def exchange(blocks):
        return [
            lax.ppermute(block, "row", [(i, (i + k + 1) % places) for i in range(places)])
            for k, block in enumerate(blocks)
        ]

    def to_owners(values):
        values = values.reshape(clusters, capacity, -1)
        return lax.all_to_all(values, OWNERS, split_axis=0, concat_axis=0, tiled=True)

    staged = stage(CHUNKS[0], block_vals, present, kept_rows)
    owners, here, staged = lax.optimization_barrier((column_owner[:, 0], present, staged))
    left_first = exchange(staged)

    hits = owners[:, None] == jnp.arange(clusters, dtype=jnp.int32)[None, :]
    index = jnp.arange(size, dtype=jnp.int32)
    before = (index[:, None] > index[None, :]).astype(jnp.bfloat16)
    earlier = jnp.dot(before, hits.astype(jnp.bfloat16), preferred_element_type=jnp.float32)
    order = jnp.sum(jnp.where(hits, earlier, 0.0), axis=1).astype(jnp.int32)
    slot_of = owners * capacity + order
    chosen = jnp.arange(slots, dtype=jnp.int32)[:, None] == slot_of[None, :]
    source = jnp.max(jnp.where(chosen, index[None, :], -1), axis=1)
    ids = jnp.where(source >= 0, (place * clusters + cluster) * size + source, -1)
    ids, here = lax.optimization_barrier((ids, here))
    arrived_ids = lax.all_to_all(
        ids.reshape(clusters, capacity), OWNERS, split_axis=0, concat_axis=0, tiled=True
    )

    left_second = exchange(stage(CHUNKS[1], block_vals, here, kept_rows))
    first = products(CHUNKS[0], present, kept_rows, slot_of, block_vals, left_first, slots)
    slot_later = lax.optimization_barrier((first, slot_of))[1]
    first = to_owners(first)
    second = to_owners(
        products(CHUNKS[1], present, kept_rows, slot_later, block_vals, left_second, slots)
    )
    arrived = [first.reshape(slots, -1), second.reshape(slots, -1)]
    pruned = finish(arrived, kept_count * size)
    return (
        pruned.reshape(1, 1, clusters, capacity, kept_count * size),
        arrived_ids.reshape(1, 1, clusters, capacity),
    )


def solution(mesh):
    placed = (
        P(("row", "col", "section"), None, None, None),
        P(("row", "col", "section"), None),
        P(),
        P(("row", "col", "section"), None),
    )
    return jax.shard_map(
        shards,
        mesh=mesh,
        in_specs=placed,
        out_specs=(
            P("row", ("col", "section"), None, None, None),
            P("row", ("col", "section"), None, None),
        ),
        check_vma=False,
    )
```
